32 devices in a mesh: groups: 2 (over x), tile: 16 (over z, y, core).
Axes of the slice: x: 2, y: 2, z: 4, core: 2. Of those that a mesh axis runs over, the one named last changes fastest.
Arguments:
- background_tokens: float32 [8192, 512], P(('groups', 'tile')), parts along dimension 0, may hold values from -6 to 6
- increment: float32 [8192, 512], P(('groups', 'tile')), parts along dimension 0, may hold values from -6 to 6
- gain_one: float32 [512], replicated, may hold values from 0.1 to 1.9
- gain_two: float32 [512], replicated, may hold values from 0.1 to 1.9
- qkv_weight: float32 [512, 1536], replicated, may hold values from -9 to 9
- out_weight: float32 [512, 512], replicated, may hold values from -0.25 to 0.25
- up_weight: float32 [512, 2048], replicated, may hold values from -0.25 to 0.25
- down_weight: float32 [2048, 512], replicated, may hold values from -0.125 to 0.125
- decoder: float32 [512, 1536], replicated, may hold values from -0.25 to 0.25
- obs_first: float32 [96, 256], replicated, may hold values from -0.625 to 0.625
- obs_second: float32 [256, 256], replicated, may hold values from -0.375 to 0.375
- obs_third: float32 [256, 32], replicated, may hold values from -0.375 to 0.375
- neighbours: int32 [4, 65536], P(None, ('groups', 'tile')), parts along dimension 1, may hold values from 0 to 65535, as said below
- interp_weights: float32 [4, 65536], P(None, ('groups', 'tile')), parts along dimension 1, may hold values from 0.1 to 0.6
- innovations: float32 [32, 65536], P(None, ('groups', 'tile')), parts along dimension 1, may hold values from -6 to 6
- obs_precision: float32 [32, 65536], P(None, ('groups', 'tile')), parts along dimension 1, may hold values from 0.3 to 3
- obs_count: int32 [32], P(('groups', 'tile')), parts along dimension 0, may hold values from 1 to 2048, as said below
Outputs:
- gradient: float32 [8192, 512], P(('groups', 'tile')), parts along dimension 0
- obs_tangent: float32 [32, 65536], P(None, ('groups', 'tile')), parts along dimension 1
The draws below stay inside these ranges and needn't reach their ends.
There are 2 independent parts, one for each index of `groups`. The reference program is written for one: setup_inputs(seed, part) draws one part's arguments, and reference() takes and returns one part's arrays. A program takes and returns all parts, laid end to end along the dimension named above; an argument that names none is the same for every part. Nothing has to cross between parts.
Inputs may be any that keep to these rules, and one draw needn't show every extreme that they name: `neighbours`: the four columns of one observation lie on one tile (one block of 4096 columns). At most 256 observation slots of one batch have their columns on one tile, and in every draw some tile holds the columns of exactly 256 slots of every batch. `obs_count`: the last batch is full.
All inputs are finite; a program needn't handle non-finite values.
Results may differ from the reference program's by a relative error of at most 0.0003.
Values sent between devices are 32-bit elements; how exact they have to be, the bound alone decides.
A program may use at most 192 MiB of HBM per device.

```python
import math
import jax
import jax.numpy as jnp
from jax import lax

D = 512
HEADS = 8
FFN = 2048
WIN = 256
SIDE = 4
PATCH = 16
COLVARS = 96
HID = 256
OUTCH = 32
TOK_DEV = 256
OBS_DEV = 2048
CAP = 256
TOKENS = 4096
COLUMNS = 65536
NOBS = 32768
N_TILE = 16


def draw_neighbours(key, part):
    key = jax.random.fold_in(key, 11)
    key_offset, key_counts, key_ranks, key_token, key_row, key_col = jax.random.split(key, 6)
    offset = jax.random.randint(key_offset, (), 0, N_TILE)
    counts = jax.random.randint(key_counts, (N_TILE, N_TILE), CAP // 2, CAP + 1)
    counts = counts.at[:, 0].set(CAP)
    bounds = jnp.cumsum(counts, axis=1)
    ranks = jax.vmap(lambda single: jax.random.permutation(single, OBS_DEV))(jax.random.split(key_ranks, N_TILE))
    section = jnp.sum((bounds[:, None, :] <= ranks[:, :, None]).astype(jnp.int32), axis=2)
    owner = (section + offset) % N_TILE
    token = jax.random.randint(key_token, (N_TILE, OBS_DEV), 0, TOK_DEV)
    patch_row = jax.random.randint(key_row, (N_TILE, OBS_DEV), 0, SIDE - 1)
    patch_col = jax.random.randint(key_col, (N_TILE, OBS_DEV), 0, SIDE - 1)
    corner = owner * (TOK_DEV * PATCH) + token * PATCH + patch_row * SIDE + patch_col
    shifts = jnp.array([0, 1, SIDE, SIDE + 1], dtype=jnp.int32)
    return (corner.reshape(-1)[None, :] + shifts[:, None]).astype(jnp.int32)


def draw_obs_count(key, part):
    key = jax.random.fold_in(key, 12)
    device = jnp.arange(N_TILE)
    rising = OBS_DEV // 3 + 2 * OBS_DEV // 3 * device // (N_TILE - 1)
    jitter = jax.random.randint(key, (N_TILE,), 0, OBS_DEV // 16 + 1)
    counts = jnp.maximum(rising - jitter, 1)
    return jnp.where(device == N_TILE - 1, OBS_DEV, counts).astype(jnp.int32)


def draw_qkv_weight(key, part):
    key = jax.random.fold_in(key, 13)
    key_base = jax.random.fold_in(key, 0)
    base = jnp.clip(jax.random.normal(key_base, (D, 3 * D), jnp.float32), -6.0, 6.0) / math.sqrt(D)
    return jnp.clip(base, -9.0, 9.0).astype(jnp.float32)


def level_of(rng, shape, cuts, low, largest):
    factor_of, own = 1.0, jax.random.fold_in(rng, 6)
    for axis_at, shards_of in cuts:
        draws = jnp.exp(jax.random.uniform(jax.random.fold_in(own, axis_at), (shards_of,), jnp.float32, low / len(cuts), largest / len(cuts)))
        factor_of = factor_of * jnp.repeat(draws, shape[axis_at] // shards_of).reshape([-1 if axis == axis_at else 1 for axis in range(len(shape))])
    return factor_of


def bell_draw(own_key, shape, deviation, most, shards=(), kind=jnp.bfloat16):
    loudness = level_of(own_key, shape, shards, -0.22, 0.18) if shards else 1.0
    values = jax.random.normal(own_key, shape, jnp.float32) * deviation * loudness
    return jnp.minimum(jnp.maximum(values, -most), most).astype(kind)


def setup_inputs(seed: int = 0, part: int = 0) -> dict:
    keys = jax.random.split(jax.random.key(seed), 18)
    part_splits = jax.random.split(jax.random.fold_in(keys[17], part), 18)
    background_tokens = bell_draw(part_splits[0], (TOKENS, D), 1.0, 6.0, ((0, 16),), jnp.float32)
    increment = bell_draw(part_splits[1], (TOKENS, D), 1.0, 6.0, ((0, 16),), jnp.float32)
    gain_one = jnp.clip(1.0 + 0.18 * jax.random.normal(keys[2], (D,), jnp.float32), 0.1, 1.9)
    gain_two = jnp.clip(1.0 + 0.18 * jax.random.normal(keys[3], (D,), jnp.float32), 0.1, 1.9)
    qkv_weight = draw_qkv_weight(jax.random.fold_in(keys[17], 71), part)
    out_weight = bell_draw(keys[5], (D, D), D ** -0.5, 0.25, (), jnp.float32)
    up_weight = bell_draw(keys[6], (D, FFN), D ** -0.5, 0.25, (), jnp.float32)
    down_weight = bell_draw(keys[7], (FFN, D), FFN ** -0.5, 0.125, (), jnp.float32)
    decoder = bell_draw(keys[8], (D, PATCH * COLVARS), D ** -0.5, 0.25, (), jnp.float32)
    obs_first = bell_draw(keys[9], (COLVARS, HID), COLVARS ** -0.5, 0.625, (), jnp.float32)
    obs_second = bell_draw(keys[10], (HID, HID), HID ** -0.5, 0.375, (), jnp.float32)
    obs_third = bell_draw(keys[11], (HID, OUTCH), HID ** -0.5, 0.375, (), jnp.float32)
    neighbours = draw_neighbours(jax.random.fold_in(jax.random.fold_in(keys[17], part), 71), part)
    interp_weights = jnp.clip(0.1 + 0.5 * jax.random.uniform(part_splits[13], (4, NOBS), jnp.float32) ** level_of(part_splits[13], (4, NOBS), ((1, 16),), -0.2, 0.2), 0.1, 0.6)
    innovations = bell_draw(part_splits[14], (OUTCH, NOBS), 1.0, 6.0, ((1, 16),), jnp.float32)
    obs_precision = jnp.clip(jnp.exp(math.log(3.0) - 2.3025851 * jax.random.uniform(part_splits[15], (OUTCH, NOBS), jnp.float32) ** level_of(part_splits[15], (OUTCH, NOBS), ((1, 16),), -0.2, 0.2)), 0.3, 3.0)
    obs_count = draw_obs_count(jax.random.fold_in(jax.random.fold_in(keys[17], part), 71), part)
    return dict(background_tokens=background_tokens, increment=increment, gain_one=gain_one, gain_two=gain_two, qkv_weight=qkv_weight, out_weight=out_weight, up_weight=up_weight, down_weight=down_weight, decoder=decoder, obs_first=obs_first, obs_second=obs_second, obs_third=obs_third, neighbours=neighbours, interp_weights=interp_weights, innovations=innovations, obs_precision=obs_precision, obs_count=obs_count)


highest = lax.Precision.HIGHEST

def product(left, right):
    return jnp.dot(left, right, precision=highest, preferred_element_type=jnp.float32)

def layer_norm(values, gain):
    centre = values - lax.optimization_barrier(jnp.mean(values, axis=-1, keepdims=True))
    spread = lax.optimization_barrier(jnp.mean(centre * centre, axis=-1, keepdims=True))
    return centre * lax.rsqrt(spread + 1e-05) * gain

def transformer(tokens, gain_one, gain_two, qkv_weight, out_weight, up_weight, down_weight):
    token_count, width = tokens.shape
    windows = token_count // WIN
    head_width = width // HEADS
    packed = product(layer_norm(tokens, gain_one), qkv_weight).reshape(windows, WIN, 3, HEADS, head_width)
    scores = jnp.einsum('wqhd,wkhd->whqk', packed[:, :, 0], packed[:, :, 1], precision=highest) / math.sqrt(head_width)
    attend = jax.nn.softmax(scores, axis=-1)
    mixed = jnp.einsum('whqk,wkhd->wqhd', attend, packed[:, :, 2], precision=highest).reshape(token_count, width)
    hidden = tokens + product(mixed, out_weight)
    inner = jax.nn.gelu(product(layer_norm(hidden, gain_two), up_weight), approximate=False)
    return hidden + product(inner, down_weight)

def linear_tangent(backward, state, direction):

    def adjoint(cotangent):
        return backward(cotangent)[0]
    unused, transpose = jax.vjp(adjoint, jnp.zeros_like(state))
    return transpose(direction)[0]

def gelu_slope(values):
    normal_cdf = 0.5 * (1.0 + lax.erf(values * 0.7071067811865476))
    return normal_cdf + values * jnp.exp(-0.5 * values * values) * 0.3989422804014327

def obs_operator(obs_first, obs_second, obs_third, base_obs, change_obs, inverse_var, innovations, scale):
    pre_one = product(base_obs, obs_first)
    slope_one = gelu_slope(pre_one)
    slope_two = gelu_slope(product(jax.nn.gelu(pre_one, approximate=False), obs_second))
    layer_two = product(product(change_obs, obs_first) * slope_one, obs_second) * slope_two
    tangent = jnp.einsum('nh,hc->cn', layer_two, obs_third, precision=highest)
    weighted = inverse_var * (tangent - innovations) * scale[None, :]
    back_two = jnp.einsum('cn,hc->nh', weighted, obs_third, precision=highest) * slope_two
    back_one = jnp.einsum('nh,ih->ni', back_two, obs_second, precision=highest) * slope_one
    return (tangent, jnp.einsum('nh,ih->ni', back_one, obs_first, precision=highest))

def reference(background_tokens, increment, gain_one, gain_two, qkv_weight, out_weight, up_weight, down_weight, decoder, obs_first, obs_second, obs_third, neighbours, interp_weights, innovations, obs_precision, obs_count):

    def model(tokens):
        return transformer(tokens, gain_one, gain_two, qkv_weight, out_weight, up_weight, down_weight)
    state, backward = jax.vjp(model, background_tokens)
    change = linear_tangent(backward, state, increment)
    base_columns = product(state, decoder).reshape(COLUMNS, COLVARS)
    change_columns = product(change, decoder).reshape(COLUMNS, COLVARS)
    base_obs = jnp.einsum('kn,knc->nc', interp_weights, base_columns[neighbours], precision=highest)
    change_obs = jnp.einsum('kn,knc->nc', interp_weights, change_columns[neighbours], precision=highest)
    slots = jnp.arange(NOBS, dtype=jnp.int32)
    live = slots % OBS_DEV < obs_count[slots // OBS_DEV]
    total = jnp.sum(obs_count.astype(jnp.float32))
    scale = jnp.where(live, 1.0, 0.0).astype(jnp.float32) * float(NOBS) / total
    obs_tangent, obs_back = obs_operator(obs_first, obs_second, obs_third, base_obs, change_obs, obs_precision, innovations, scale)
    spread_back = (interp_weights[:, :, None] * obs_back[None, :, :]).reshape(-1, COLVARS)
    column_back = jnp.zeros((COLUMNS, COLVARS), jnp.float32).at[neighbours.reshape(-1)].add(spread_back)
    state_back = product(column_back.reshape(TOKENS, PATCH * COLVARS), decoder.T)
    gradient = increment + backward(state_back)[0]
    return (gradient, obs_tangent)
```

```python
import functools
import math

import jax
import jax.numpy as jnp
from jax import lax
from jax.experimental import pallas as pl
from jax.experimental.pallas import tpu as pltpu
from jax.sharding import PartitionSpec as P

HEADS = 8
WIN = 256
PATCH = 16
ROWS = 80
f32 = jnp.float32
bf16 = jnp.bfloat16
high = lax.Precision.HIGH
highest = lax.Precision.HIGHEST
NN = (((1,), (0,)), ((), ()))
NT = (((1,), (1,)), ((), ()))


def product(left, right, precision=high):
    return jnp.dot(left, right, precision=precision, preferred_element_type=f32)


def layer_norm(values, gain):
    centre = values - jnp.mean(values, axis=-1, keepdims=True)
    spread = jnp.mean(centre * centre, axis=-1, keepdims=True)
    return centre * lax.rsqrt(spread + 1e-05) * gain


def transformer(tokens, gain_one, gain_two, qkv_weight, out_weight, up_weight, down_weight):
    token_count, width = tokens.shape
    windows = token_count // WIN
    head_width = width // HEADS
    packed = product(layer_norm(tokens, gain_one), qkv_weight, highest).reshape(
        windows, WIN, 3, HEADS, head_width
    )
    scores = jnp.einsum(
        "wqhd,wkhd->whqk", packed[:, :, 0], packed[:, :, 1], precision=highest
    ) / math.sqrt(head_width)
    attend = jax.nn.softmax(scores, axis=-1)
    mixed = jnp.einsum("whqk,wkhd->wqhd", attend, packed[:, :, 2], precision=high).reshape(
        token_count, width
    )
    hidden = tokens + product(mixed, out_weight)
    inner = jax.nn.gelu(product(layer_norm(hidden, gain_two), up_weight), approximate=False)
    return hidden + product(inner, down_weight)


def split(values):
    top = values.astype(bf16)
    return top, (values - top.astype(f32)).astype(bf16)


def dot(left, right, dims=NN):
    return lax.dot_general(left, right, dims, preferred_element_type=f32)


def dot3(left, right, dims=NN):
    left_top, left_low = left if isinstance(left, tuple) else split(left)
    right_top, right_low = right if isinstance(right, tuple) else split(right)
    return (
        dot(left_top, right_top, dims)
        + dot(left_low, right_top, dims)
        + dot(left_top, right_low, dims)
    )


def pack_kernel(
    tiles, cap, tokens, count_ref, near_ref, interp_ref, innov_ref, prec_ref,
    packet_ref, target_ref, halves,
):
    tile = pl.program_id(0)
    slots = near_ref.shape[1]
    col_rows = tokens * PATCH

    @pl.when(tile == 0)
    def prepare():
        near = near_ref[...]
        owner = near[0:1, :] // col_rows
        local = near - owner * col_rows
        token = local // PATCH
        place = ((local - token * PATCH) * tokens + token).astype(f32)
        member = lax.broadcasted_iota(jnp.int32, (tiles, slots), 0) == owner
        chosen = jnp.where(member, 1.0, 0.0).astype(f32)
        step = 256
        before = lax.broadcasted_iota(jnp.int32, (step, step), 0)
        after = lax.broadcasted_iota(jnp.int32, (step, step), 1)
        triangle = jnp.where(before < after, 1.0, 0.0).astype(bf16)
        carry = jnp.zeros((tiles, 1), f32)
        for start in range(0, slots, step):
            part = chosen[:, start : start + step]
            ahead = dot(part.astype(bf16), triangle) + carry
            rank = jnp.sum(part * ahead, axis=0, keepdims=True)
            target_ref[:, start : start + step] = (
                owner[:, start : start + step] * cap + rank.astype(jnp.int32)
            )
            carry = carry + jnp.sum(part, axis=1, keepdims=True)
        count = count_ref[0]
        live = lax.broadcasted_iota(jnp.int32, (1, slots), 1) < count
        small = jnp.concatenate([place, interp_ref[...]], axis=0)
        weight = prec_ref[...] * jnp.where(live, 1.0, 0.0)
        rest = jnp.zeros((ROWS - 8 - 2 * prec_ref.shape[0], slots), f32)
        whole = jnp.concatenate([small, innov_ref[...], weight, rest], axis=0)
        top, low = split(whole)
        halves[0:ROWS, :] = top
        halves[ROWS : 2 * ROWS, :] = low

    wanted = lax.broadcasted_iota(jnp.int32, (cap, slots), 0) + tile * cap
    onehot = jnp.where(wanted == target_ref[...], 1.0, 0.0).astype(bf16)
    moved = dot(halves[...], onehot, NT)
    row = lax.broadcasted_iota(jnp.int32, (ROWS, cap), 0)
    packet_ref[0] = jnp.where(
        row == ROWS - 1, count_ref[0].astype(f32), moved[:ROWS] + moved[ROWS:]
    )


def gelu_parts(values):
    cdf = 0.5 * (1.0 + lax.erf(values * 0.7071067811865476))
    slope = cdf + values * jnp.exp(-0.5 * values * values) * 0.3989422804014327
    return values * cdf, slope


def obs_kernel(
    tokens, colvars, channels, scale_ref, packet_ref, base_ref, change_ref,
    first_ref, first_t_ref, second_ref, second_t_ref, third_ref, third_t_ref,
    tangent_ref, back_ref, left, wide_top, wide_low,
):
    cap = packet_ref.shape[2]

    @pl.when(pl.program_id(0) == 0)
    def prepare():
        for patch in range(PATCH):
            rows = slice(patch * colvars, (patch + 1) * colvars)
            base_top, base_low = split(base_ref[rows, :])
            change_top, change_low = split(change_ref[rows, :])
            left[patch, 0:colvars, :] = base_top
            left[patch, colvars : 2 * colvars, :] = change_top
            left[patch, 2 * colvars : 3 * colvars, :] = base_low
            left[patch, 3 * colvars : 4 * colvars, :] = change_low
        back_ref[...] = jnp.zeros_like(back_ref)

    place = [packet_ref[0, k : k + 1, :].astype(jnp.int32) for k in range(4)]
    weight = [packet_ref[0, 4 + k : 5 + k, :] for k in range(4)]
    for k in range(1, 4):
        for j in range(k):
            same = place[k] == place[j]
            weight[j] = weight[j] + jnp.where(same, weight[k], 0.0)
            weight[k] = jnp.where(same, 0.0, weight[k])
            place[k] = jnp.where(same, -1, place[k])

    row = lax.broadcasted_iota(jnp.int32, (tokens, cap), 0)

    def gather(patch, sums):
        full, part = sums
        chosen = jnp.zeros((tokens, cap), f32)
        for k in range(4):
            chosen = jnp.where(row == place[k] - patch * tokens, weight[k], chosen)
        top, low = split(chosen)
        wide_top[patch] = top
        wide_low[patch] = low
        return full + dot(left[patch], top), part + dot(left[patch, : 2 * colvars, :], low)

    full, part = lax.fori_loop(
        0,
        PATCH,
        gather,
        (jnp.zeros((4 * colvars, cap), f32), jnp.zeros((2 * colvars, cap), f32)),
        unroll=2,
    )
    both = full[: 2 * colvars] + full[2 * colvars :] + part
    base, change = both[:colvars], both[colvars:]
    first_t = split(first_t_ref[...])
    second_t = split(second_t_ref[...])
    active, slope_one = gelu_parts(dot3(first_t, base))
    slope_two = gelu_parts(dot3(second_t, active))[1]
    layer_two = dot3(second_t, dot3(first_t, change) * slope_one) * slope_two
    tangent = dot3(third_t_ref[...], layer_two)
    tangent_ref[0] = tangent
    innov = packet_ref[0, 8 : 8 + channels, :]
    prec = packet_ref[0, 8 + channels : 8 + 2 * channels, :]
    weighted = prec * (tangent - innov) * scale_ref[0]
    back_two = dot3(third_ref[...], weighted) * slope_two
    back_one = dot3(second_ref[...], back_two) * slope_one
    top, low = split(dot3(first_ref[...], back_one))
    stacked = jnp.concatenate([top, low], axis=0)

    def scatter(patch, unused):
        full = dot(stacked, wide_top[patch], NT)
        part = dot(top, wide_low[patch], NT)
        start = pl.multiple_of(patch * colvars, colvars)
        back_ref[pl.ds(start, colvars), :] += full[:colvars] + full[colvars:] + part
        return unused

    lax.fori_loop(0, PATCH, scatter, 0, unroll=2)


def unpack_kernel(cap, target_ref, arrived_ref, out_ref):
    tile = pl.program_id(0)
    slots = target_ref.shape[1]
    channels = arrived_ref.shape[1]
    wanted = lax.broadcasted_iota(jnp.int32, (cap, slots), 0) + tile * cap
    onehot = jnp.where(wanted == target_ref[...], 1.0, 0.0).astype(bf16)
    stacked = jnp.concatenate(split(arrived_ref[0]), axis=0)
    moved = dot(stacked, onehot)
    moved = moved[:channels] + moved[channels:]

    @pl.when(tile == 0)
    def begin():
        out_ref[...] = moved

    @pl.when(tile > 0)
    def add():
        out_ref[...] += moved


def whole_spec(array):
    rank = array.ndim
    return pl.BlockSpec(array.shape, lambda j: (0,) * rank)


def params():
    return pltpu.CompilerParams(vmem_limit_bytes=48 * 1024 * 1024)


def on_device(
    background_tokens,
    increment,
    gain_one,
    gain_two,
    qkv_weight,
    out_weight,
    up_weight,
    down_weight,
    decoder,
    obs_first,
    obs_second,
    obs_third,
    neighbours,
    interp_weights,
    innovations,
    obs_precision,
    obs_count,
):
    tiles = lax.axis_size("tile")
    slots = neighbours.shape[1]
    cap = 2 * slots // tiles
    tokens = background_tokens.shape[0]
    colvars = decoder.shape[1] // PATCH
    channels = innovations.shape[0]
    smem = pl.BlockSpec(memory_space=pltpu.SMEM)

    packets, target = pl.pallas_call(
        functools.partial(pack_kernel, tiles, cap, tokens),
        grid=(tiles,),
        in_specs=[smem]
        + [whole_spec(a) for a in (neighbours, interp_weights, innovations, obs_precision)],
        out_specs=[
            pl.BlockSpec((1, ROWS, cap), lambda j: (j, 0, 0)),
            pl.BlockSpec((1, slots), lambda j: (0, 0)),
        ],
        out_shape=[
            jax.ShapeDtypeStruct((tiles, ROWS, cap), f32),
            jax.ShapeDtypeStruct((1, slots), jnp.int32),
        ],
        scratch_shapes=[pltpu.VMEM((2 * ROWS, slots), bf16)],
        compiler_params=params(),
        name="pack",
    )(obs_count, neighbours, interp_weights, innovations, obs_precision)
    arrived = lax.all_to_all(packets, "tile", split_axis=0, concat_axis=0, tiled=True)
    total = jnp.sum(arrived[:, ROWS - 1, 0])
    scale = (float(slots * tiles) / total).reshape(1)

    def model(values):
        return transformer(
            values, gain_one, gain_two, qkv_weight, out_weight, up_weight, down_weight
        )

    state, backward = jax.vjp(model, background_tokens)
    change = jax.jvp(model, (background_tokens,), (increment,))[1]
    decode = lambda values: lax.dot_general(
        decoder, values, (((0,), (1,)), ((), ())), precision=high, preferred_element_type=f32
    )
    operands = (
        arrived, decode(state), decode(change), obs_first, obs_first.T, obs_second,
        obs_second.T, obs_third, obs_third.T,
    )
    tangent, column_back = pl.pallas_call(
        functools.partial(obs_kernel, tokens, colvars, channels),
        grid=(tiles,),
        in_specs=[smem, pl.BlockSpec((1, ROWS, cap), lambda j: (j, 0, 0))]
        + [whole_spec(a) for a in operands[1:]],
        out_specs=[
            pl.BlockSpec((1, channels, cap), lambda j: (j, 0, 0)),
            pl.BlockSpec((PATCH * colvars, tokens), lambda j: (0, 0)),
        ],
        out_shape=[
            jax.ShapeDtypeStruct((tiles, channels, cap), f32),
            jax.ShapeDtypeStruct((PATCH * colvars, tokens), f32),
        ],
        scratch_shapes=[
            pltpu.VMEM((PATCH, 4 * colvars, tokens), bf16),
            pltpu.VMEM((PATCH, tokens, cap), bf16),
            pltpu.VMEM((PATCH, tokens, cap), bf16),
        ],
        compiler_params=params(),
        name="observe",
    )(scale, *operands)
    returned = lax.all_to_all(tangent, "tile", split_axis=0, concat_axis=0, tiled=True)
    state_back = lax.dot_general(
        column_back, decoder, (((0,), (1,)), ((), ())), precision=high, preferred_element_type=f32
    )
    gradient = increment + backward(state_back)[0]
    obs_tangent = pl.pallas_call(
        functools.partial(unpack_kernel, cap),
        grid=(tiles,),
        in_specs=[
            pl.BlockSpec((1, slots), lambda j: (0, 0)),
            pl.BlockSpec((1, channels, cap), lambda j: (j, 0, 0)),
        ],
        out_specs=pl.BlockSpec((channels, slots), lambda j: (0, 0)),
        out_shape=jax.ShapeDtypeStruct((channels, slots), f32),
        compiler_params=params(),
        name="unpack",
    )(target, returned)
    return (gradient, obs_tangent)


def solution(mesh):
    every = ("groups", "tile")
    in_specs = (
        (P(every, None),) * 2 + (P(),) * 10 + (P(None, every),) * 4 + (P(every),)
    )
    out_specs = (P(every, None), P(None, every))
    return jax.shard_map(
        on_device, mesh=mesh, in_specs=in_specs, out_specs=out_specs, check_vma=False
    )
```
